32 devices in a mesh: sub: 8 (over z, core), dom: 4 (over y, x).
Axes of the slice: x: 2, y: 2, z: 4, core: 2. Of those that a mesh axis runs over, the one named last changes fastest.
Arguments:
- start_vectors: float32 [8, 3, 64, 4, 16, 128], P('sub', None, None, 'dom'), may hold values from -6 to 6
- face_x: float32 [8, 4, 16, 128], P('sub', 'dom'), may hold values from 0.1 to 10
- face_y: float32 [8, 4, 16, 128], P('sub', 'dom'), may hold values from 0.1 to 10
- face_z: float32 [8, 4, 16, 128], P('sub', 'dom'), may hold values from 0.1 to 10
- masses: float32 [8, 4, 16, 128], P('sub', 'dom'), may hold values from 0.5 to 2
- active: int32 [8], P('sub'), may hold values from 8 to 16, as said below
Outputs:
- deflation: bfloat16 [8, 3, 64, 4, 16, 128], P('sub', None, None, 'dom')
- coarse_diag: float32 [8, 64, 64], P('sub')
- coarse_off: float32 [8, 64, 64], P('sub')
The draws below stay inside these ranges and needn't reach their ends.
Inputs may be any that keep to these rules, and one draw needn't show every extreme that they name: `active`: some subdomain has all 16 planes.
All inputs are finite; a program needn't handle non-finite values.
Results may differ from the reference program's by a relative error of at most 0.001.
Values sent between devices are 32-bit elements; how exact they have to be, the bound alone decides.
A program may use at most 64 MiB of HBM per device.

```python
import math
import jax
import jax.numpy as jnp
from jax import lax

K = 64
NXS = 16
NZ = 128
OV = 4
STEPS = 2
SUBS = 8
NY = 4


def draw_active(key, part):
    base = jax.random.fold_in(key, 7)
    first_key, second_key = jax.random.split(base)
    counts = jax.random.randint(first_key, (SUBS,), NXS // 2, NXS + 1, dtype=jnp.int32)
    chosen = jax.random.randint(second_key, (), 0, SUBS, dtype=jnp.int32)
    return jnp.where(jnp.arange(SUBS, dtype=jnp.int32) == chosen, NXS, counts).astype(jnp.int32)


def steps_of(rng, dims, cuts, least, high):
    gain, own = 1.0, jax.random.fold_in(rng, 6)
    for dim, parts in cuts:
        draws = jnp.exp(jax.random.uniform(jax.random.fold_in(own, dim), (parts,), jnp.float32, least / len(cuts), high / len(cuts)))
        gain = gain * jnp.repeat(draws, dims[dim] // parts).reshape([-1 if axis == dim else 1 for axis in range(len(dims))])
    return gain


def bell_draw(key, shape, width, reach, cuts=(), held_as=jnp.bfloat16):
    gain = steps_of(key, shape, cuts, -0.22, 0.18) if cuts else 1.0
    drawn = jax.random.normal(key, shape, jnp.float32) * width * gain
    return jnp.minimum(jnp.maximum(drawn, -reach), reach).astype(held_as)


def setup_inputs(seed: int = 0) -> dict:
    arg_keys = jax.random.split(jax.random.key(seed), 7)
    return {
        "start_vectors": bell_draw(arg_keys[0], (SUBS, 3, K, NY, NXS, NZ), 1.0, 6.0, ((0, 8), (3, 4)), jnp.float32),
        "face_x": jnp.clip(jnp.exp(math.log(10.0) - 4.6051702 * jax.random.uniform(arg_keys[1], (SUBS, NY, NXS, NZ), jnp.float32) ** steps_of(arg_keys[1], (SUBS, NY, NXS, NZ), ((0, 8), (1, 4)), -0.2, 0.2)), 0.1, 10.0),
        "face_y": jnp.clip(jnp.exp(math.log(10.0) - 4.6051702 * jax.random.uniform(arg_keys[2], (SUBS, NY, NXS, NZ), jnp.float32) ** steps_of(arg_keys[2], (SUBS, NY, NXS, NZ), ((0, 8), (1, 4)), -0.2, 0.2)), 0.1, 10.0),
        "face_z": jnp.clip(jnp.exp(math.log(10.0) - 4.6051702 * jax.random.uniform(arg_keys[3], (SUBS, NY, NXS, NZ), jnp.float32) ** steps_of(arg_keys[3], (SUBS, NY, NXS, NZ), ((0, 8), (1, 4)), -0.2, 0.2)), 0.1, 10.0),
        "masses": jnp.clip(jnp.exp(math.log(2.0) - 1.3862944 * jax.random.uniform(arg_keys[4], (SUBS, NY, NXS, NZ), jnp.float32) ** steps_of(arg_keys[4], (SUBS, NY, NXS, NZ), ((0, 8), (1, 4)), -0.2, 0.2)), 0.5, 2.0),
        "active": draw_active(jax.random.fold_in(arg_keys[6], 71), 0),
    }


def gram_of(left, right):
    return jnp.einsum('ckyxz,clyxz->kl', left, right, precision=lax.Precision.HIGHEST)

def mix_cols(values, matrix):
    return jnp.einsum('ckyxz,kl->clyxz', values, matrix, precision=lax.Precision.HIGHEST)

def inverse_factor(gram_b):
    factor = jnp.linalg.cholesky(gram_b)
    identity = jnp.eye(gram_b.shape[0], dtype=jnp.float32)
    return lax.linalg.triangular_solve(factor, identity, left_side=True, lower=True)

def face_terms(values, weights, along):
    length = values.shape[along]
    head_part = lax.slice_in_dim(values, 0, length - 1, axis=along)
    tail_part = lax.slice_in_dim(values, 1, length, axis=along)
    fluxes = lax.slice_in_dim(weights, 0, length - 1, axis=along - 2)[None, None] * (head_part - tail_part)
    pad_after = [(0, 0)] * 5
    pad_after[along] = (0, 1)
    pad_before = [(0, 0)] * 5
    pad_before[along] = (1, 0)
    return jnp.pad(fluxes, pad_after) - jnp.pad(fluxes, pad_before)

def lower_faces(weights, along):
    length = weights.shape[along]
    widths = [(0, 0)] * 3
    widths[along] = (1, 0)
    return jnp.pad(lax.slice_in_dim(weights, 0, length - 1, axis=along), widths)

def operate(values, live_x, live_y, live_z):
    return face_terms(values, live_y, 2) + face_terms(values, live_x, 3) + face_terms(values, live_z, 4)

def one_domain(start, face_x, face_y, face_z, masses, active):
    row_index = jnp.arange(NY, dtype=jnp.int32)
    plane_index = jnp.arange(NXS, dtype=jnp.int32)
    depth_index = jnp.arange(NZ, dtype=jnp.int32)
    inside = (plane_index < active)[None, :, None]
    keep_x = (plane_index + 1 < active)[None, :, None]
    keep_y = inside & (row_index + 1 < NY)[:, None, None]
    keep_z = inside & (depth_index + 1 < NZ)[None, None, :]
    live_x = face_x * keep_x.astype(jnp.float32)
    live_y = face_y * keep_y.astype(jnp.float32)
    live_z = face_z * keep_z.astype(jnp.float32)
    diagonal = live_x + lower_faces(live_x, 1) + live_y + lower_faces(live_y, 0) + live_z + lower_faces(live_z, 2) + masses
    unity = jnp.clip(jnp.minimum(plane_index + 1, active - plane_index).astype(jnp.float32) / (OV + 1), 0.0, 1.0)[None, :, None]
    b_weight = masses * unity * unity
    vectors = start * inside.astype(jnp.float32)[None, None]
    for repeat in range(STEPS):
        inv_now = inverse_factor(gram_of(vectors, b_weight[None, None] * vectors))
        ortho = mix_cols(vectors, inv_now.T)
        image = operate(ortho, live_x, live_y, live_z)
        rayleigh = gram_of(ortho, image)
        residual = image - mix_cols(b_weight[None, None] * ortho, rayleigh)
        vectors = ortho - 0.5 * residual / diagonal[None, None]
    inv_now = inverse_factor(gram_of(vectors, b_weight[None, None] * vectors))
    deflate = unity[None, None] * mix_cols(vectors, inv_now.T)
    image = operate(deflate, live_x, live_y, live_z)
    coarse = gram_of(deflate, image)
    first_planes = deflate[:, :, :, :OV]
    last_planes = lax.dynamic_slice_in_dim(image, (active - OV).astype(jnp.int32), OV, axis=3)
    return (deflate.astype(jnp.bfloat16), coarse, first_planes, last_planes)

def reference(start_vectors, face_x, face_y, face_z, masses, active):
    deflation, coarse_diag, first_planes, last_planes = lax.map(lambda packed: one_domain(*packed), (start_vectors, face_x, face_y, face_z, masses, active))
    previous = jnp.concatenate([jnp.zeros_like(last_planes[:1]), last_planes[:-1]], axis=0)
    coarse_off = jnp.einsum('sckyxz,sclyxz->skl', first_planes, previous, precision=lax.Precision.HIGHEST)
    return (deflation, coarse_diag, coarse_off)
```

```python
import functools

import jax
import jax.numpy as jnp
from jax import lax
from jax.experimental import pallas as pl
from jax.experimental.pallas import tpu as pltpu
from jax.sharding import PartitionSpec as P

OV = 4
STEPS = 2
MESH = pl.DeviceIdType.MESH
F32 = jnp.float32
BF16 = jnp.bfloat16


def split(v):
    hi = v.astype(BF16)
    return hi, (v - hi.astype(F32)).astype(BF16)


def nt(a, b):
    return lax.dot_general(a, b, (((1,), (1,)), ((), ())), preferred_element_type=F32)


def exact(a, b, dims):
    return lax.dot_general(
        a, b, (dims, ((), ())), precision=lax.Precision.HIGHEST, preferred_element_type=F32
    )


def kernel(
    n, subs, comps, nk, nx,
    start, fx, fy, fz, mass, active,
    out, diag_out, off_out,
    sbuf, vec, img, home, rows32, cs, cr, dv, hs, hr, gr, gf, us, ur, fs, fr,
    s_sem, r_sem, cs_sem, cr_sem, hs_sem, hr_sem, gs_sem, gr_sem,
    ws_sem, wr_sem, us_sem, ur_sem,
):
    nz = fx.shape[1]
    group = nz // n
    nq = nx // n
    per = n * comps
    me = lax.axis_index("dom")
    sub = lax.axis_index("sub")
    peers = [lax.rem(me + d, n) for d in range(n)]
    right, left = peers[1], peers[n - 1]
    next_sub, prev_sub = lax.rem(sub + 1, subs), lax.rem(sub + subs - 1, subs)

    barrier = pltpu.get_barrier_semaphore()
    for d in range(1, n):
        pl.semaphore_signal(barrier, inc=1, device_id=(sub, peers[d]), device_id_type=MESH)
    for s in (next_sub, prev_sub):
        pl.semaphore_signal(barrier, inc=1, device_id=(s, me), device_id_type=MESH)

    a = active[0]
    lane = lax.broadcasted_iota(jnp.int32, (1, nz), 1)
    grp = lane // group
    zin = lane - grp * group

    pi = lax.broadcasted_iota(jnp.int32, (nx, nz), 0)
    zi = lax.broadcasted_iota(jnp.int32, (nx, nz), 1)
    kx = jnp.where(pi + 1 < a, fx[...], 0.0)
    ky = jnp.where((pi < a) & (me + 1 < n), fy[...], 0.0)
    kz = jnp.where((pi < a) & (zi + 1 < nz), fz[...], 0.0)
    lx = jnp.where(pi == 0, 0.0, pltpu.roll(kx, 1, 0))
    lz = jnp.where(zi == 0, 0.0, pltpu.roll(kz, 1, 1))
    coefs = (kx, lx, ky, kz, lz, mass[...])

    def regroup(blocks, e):
        res = blocks[0]
        for r in range(1, n):
            res = jnp.where(grp == lax.rem(e + r, n), blocks[r], res)
        return pltpu.roll(res, lax.rem(n - e, n) * group, 1)

    for ai, arr in enumerate(coefs):
        for q in range(nq):
            blocks = [
                pltpu.roll(jnp.broadcast_to(arr[q * n + r : q * n + r + 1], (8, nz)), r * group, 1)
                for r in range(n)
            ]
            for d in range(n):
                res = regroup(blocks, peers[d])
                if d == 0:
                    cr[me, ai, q] = res
                else:
                    cs[d, ai, q] = res

    pl.semaphore_wait(barrier, n - 1 + 2)

    def to_peer(src, dst, ss, rs, d):
        return pltpu.make_async_remote_copy(
            src_ref=src, dst_ref=dst, send_sem=ss, recv_sem=rs,
            device_id=(sub, peers[d]), device_id_type=MESH,
        )

    def to_next(src, dst, ss, rs):
        return pltpu.make_async_remote_copy(
            src_ref=src, dst_ref=dst, send_sem=ss, recv_sem=rs,
            device_id=(next_sub, me), device_id_type=MESH,
        )

    coef_copies = [
        to_peer(cs.at[d], cr.at[me], cs_sem.at[d], cr_sem.at[d], d) for d in range(1, n)
    ]
    for cp in coef_copies:
        cp.start()

    vec_copies = []
    for c in range(comps):
        def pack(q, _, c=c):
            blocks = []
            for r in range(n):
                x = q * n + r
                v = start[c, pl.ds(x, nk, stride=nx), :]
                blocks.append(pltpu.roll(jnp.where(x < a, v, 0.0), r * group, 1))
            for d in range(n):
                res = regroup(blocks, peers[d])
                if d == 0:
                    vec[me, c, q] = res
                else:
                    sbuf[d, c, q] = res
            return 0
        lax.fori_loop(0, nq, pack, 0)
        for d in range(1, n):
            cp = to_peer(sbuf.at[d, c], vec.at[me, c], s_sem.at[c, d], r_sem.at[c, d], d)
            cp.start()
            vec_copies.append(cp)

    for cp in coef_copies:
        cp.wait()

    for y in range(n):
        for q in range(nq):
            plane = q * n + grp
            ckx, clx, cky, ckz, clz, cm = (cr[y, ai, q] for ai in range(6))
            ly = cr[y - 1, 2, q] if y else jnp.zeros_like(cky)
            total = ckx + clx + cky + ly + ckz + clz
            unity = jnp.clip(
                jnp.minimum(plane + 1, a - plane).astype(F32) / (OV + 1), 0.0, 1.0
            )
            unity = jnp.broadcast_to(unity, total.shape)
            half = 0.5 / (total + cm)
            b = cm * unity * unity
            tail = ((plane >= a - OV) & (plane < a)).astype(F32)
            for i, arr in enumerate((total, ly, half, half * b, b, unity, jnp.broadcast_to(tail, total.shape))):
                dv[i, y, q] = arr

    for cp in vec_copies:
        cp.wait()

    def halo_copies(p):
        return (
            to_peer(hs.at[p, 0], hr.at[p, 0], hs_sem.at[p, 0], hr_sem.at[p, 0], n - 1),
            to_peer(hs.at[p, 1], hr.at[p, 1], hs_sem.at[p, 1], hr_sem.at[p, 1], 1),
        )

    def put_halo(p, y, c, q, v):
        b = (y * comps + c) * nq + q
        slot = lax.div(b, group)
        pos = b - slot * group
        lo = pltpu.roll(v, pos, 1)
        hi = pltpu.roll(v, lax.rem(pos + nz + 1 - group, nz), 1)
        here = zin == pos
        hs[p, 0, slot] = jnp.where(here, lo, hs[p, 0, slot])
        hs[p, 1, slot] = jnp.where(here, hi, hs[p, 1, slot])

    def row(ref, i, y, q):
        return ref[i, y, q][0:1]

    def apply_and_gram(p):
        def body(i, acc):
            y = lax.div(i, comps)
            c = i - y * comps
            yu, yd = jnp.minimum(y + 1, n - 1), jnp.maximum(y - 1, 0)
            vs = [vec[y, c, q] for q in range(nq)]
            ups = [pltpu.roll(v, nz - group, 1) for v in vs]
            downs = [pltpu.roll(v, group, 1) for v in vs]
            lefts, bvs = [], []
            for q in range(nq):
                v = vs[q]
                b = i * nq + q
                slot = lax.div(b, group)
                pos = b - slot * group
                xp = ups[q] if q + 1 == nq else jnp.where(grp == n - 1, ups[q + 1], ups[q])
                xm = downs[q] if q == 0 else jnp.where(grp == 0, downs[q - 1], downs[q])
                zp = jnp.where(
                    zin == group - 1, pltpu.roll(hr[p, 0, slot], group - 1 - pos, 1),
                    pltpu.roll(v, nz - 1, 1),
                )
                zm = jnp.where(
                    zin == 0, pltpu.roll(hr[p, 1, slot], lax.rem(nz - pos, nz), 1),
                    pltpu.roll(v, 1, 1),
                )
                def cf(ai):
                    return cr[y, ai, q][0:1]
                res = (
                    row(dv, 0, y, q) * v
                    - cf(0) * xp - cf(1) * xm
                    - cf(2) * vec[yu, c, q] - row(dv, 1, y, q) * vec[yd, c, q]
                    - cf(3) * zp - cf(4) * zm
                )
                img[y, c, q] = res
                lefts.append(res)
                bvs.append(v * (cf(5) if p == STEPS else row(dv, 4, y, q)))
            v_hi, v_lo = split(jnp.concatenate(vs, 1))
            b_hi, b_lo = split(jnp.concatenate(bvs, 1))
            a_hi, a_lo = split(jnp.concatenate(lefts, 1))
            return acc + nt(
                jnp.concatenate([v_hi, v_lo], 0),
                jnp.concatenate([b_hi, a_hi, b_lo, a_lo], 0),
            )

        acc = lax.fori_loop(0, per, body, jnp.zeros((2 * nk, 4 * nk), F32))
        return acc[:nk, : 2 * nk] + acc[:nk, 2 * nk :] + acc[nk:, : 2 * nk]

    def gather(ref, sems, make):
        copies = [
            to_peer(ref.at[me], ref.at[me], sems[0].at[d], sems[1].at[d], d) for d in range(1, n)
        ]
        for cp in copies:
            cp.start()
        for cp in copies:
            cp.wait()
        total = ref[0]
        for y in range(1, n):
            total = total + ref[y]
        return total

    hs[...] = jnp.zeros_like(hs)
    ri = lax.broadcasted_iota(jnp.int32, (nk, 1), 0)

    def pack_halo(i, _):
        y = lax.div(i, comps)
        c = i - y * comps
        for q in range(nq):
            put_halo(0, y, c, q, vec[y, c, q])
        return 0

    lax.fori_loop(0, per, pack_halo, 0)

    for p in range(STEPS):
        copies = halo_copies(p)
        for cp in copies:
            cp.start()
        for cp in copies:
            cp.wait()
        gr[p, me] = apply_and_gram(p)
        m = gather(gr.at[p], (gs_sem.at[p], gr_sem.at[p]), None)
        for j in range(nk):
            piv = m[j : j + 1, j : j + 1]
            line = m[j : j + 1, :] / piv
            m = jnp.where(ri == j, line, m - m[:, j : j + 1] * line)
        xt = m.T[nk:, :]
        x_hi, x_lo = split(xt)
        x3 = jnp.concatenate([x_hi, x_lo, x_hi], 1)

        def update(i, _, p=p, x3=x3):
            y = lax.div(i, comps)
            c = i - y * comps
            v = jnp.concatenate([vec[y, c, q] for q in range(nq)], 1)
            v_hi, v_lo = split(v)
            mixed = jnp.dot(
                x3, jnp.concatenate([v_hi, v_hi, v_lo], 0), preferred_element_type=F32
            )
            for q in range(nq):
                new = (
                    vec[y, c, q]
                    - row(dv, 2, y, q) * img[y, c, q]
                    + row(dv, 3, y, q) * mixed[:, q * nz : (q + 1) * nz]
                )
                if p == STEPS - 1:
                    new = new * row(dv, 5, y, q)
                vec[y, c, q] = new
                put_halo(p + 1, y, c, q, new)
            return 0

        lax.fori_loop(0, per, update, 0)

    copies = halo_copies(STEPS)
    for cp in copies:
        cp.start()
    back = []
    for d in range(1, n):
        cp = to_peer(vec.at[peers[d]], home.at[me], ws_sem.at[d], wr_sem.at[d], d)
        cp.start()
        back.append(cp)
    for cp in copies:
        cp.wait()
    both = apply_and_gram(STEPS)

    r0 = lax.rem(a - OV, n)

    def planes(i, _):
        y = lax.div(i, comps)
        c = i - y * comps
        u = img[y, c, 0] * row(dv, 6, y, 0)
        for q in range(1, nq):
            u = u + img[y, c, q] * row(dv, 6, y, q)
        bit = 1
        while bit < n:
            moved = pltpu.roll(u, nz - bit * group, 1)
            u = jnp.where(lax.rem(lax.div(r0, bit), 2) == 1, moved, u)
            bit *= 2
        us[y, c] = u
        return 0

    lax.fori_loop(0, per, planes, 0)
    ucopy = to_next(us, ur, us_sem.at[0], ur_sem.at[0])
    ucopy.start()
    ucopy.wait()

    def off_body(i, acc):
        y = lax.div(i, comps)
        c = i - y * comps
        w_hi, w_lo = split(jnp.where(grp < OV, vec[y, c, 0], 0.0))
        u_hi, u_lo = split(ur[y, c])
        return acc + nt(jnp.concatenate([w_hi, w_lo], 0), jnp.concatenate([u_hi, u_lo], 0))

    off = lax.fori_loop(0, per, off_body, jnp.zeros((2 * nk, 2 * nk), F32))
    off = off[:nk, :nk] + off[nk:, :nk] + off[:nk, nk:]
    gf[me, 0] = both
    gf[me, 1] = jnp.concatenate([off, jnp.zeros_like(off)], 1)
    grams = gather(gf, (gs_sem.at[STEPS], gr_sem.at[STEPS]), None)

    eye = (lax.broadcasted_iota(jnp.int32, (nk, 2 * nk), 0) + nk
           == lax.broadcasted_iota(jnp.int32, (nk, 2 * nk), 1)).astype(F32)
    right_half = lax.broadcasted_iota(jnp.int32, (nk, 2 * nk), 1) >= nk
    m = jnp.where(right_half, eye, grams[0])
    for j in range(nk):
        piv = m[j : j + 1, j : j + 1]
        line = m[j : j + 1, :]
        inv = 1.0 / piv
        m = jnp.where(
            ri > j, m - m[:, j : j + 1] * (line * inv), jnp.where(ri == j, line * lax.rsqrt(piv), m)
        )
    factor = m[:, nk:]
    fs[...] = m
    fcopy = to_next(fs, fr, us_sem.at[1], ur_sem.at[1])
    fcopy.start()
    diag_out[...] = exact(
        exact(factor, grams[0][:, nk:], ((1,), (0,))), factor, ((1,), (1,))
    )
    half_off = exact(factor, grams[1][:, :nk], ((1,), (0,)))

    for y_cp in back:
        y_cp.wait()
    f_hi, f_lo = split(factor)
    f3 = jnp.concatenate([f_hi, f_lo, f_hi], 1)
    home[me] = vec[me]

    def finish(i, _):
        c = lax.div(i, nq)
        q = i - c * nq
        w = jnp.concatenate([home[e, c, q] for e in range(n)], 1)
        w_hi, w_lo = split(w)
        z = jnp.dot(f3, jnp.concatenate([w_hi, w_hi, w_lo], 0), preferred_element_type=F32)
        blocks = [pltpu.roll(z[:, e * nz : (e + 1) * nz], e * group, 1) for e in range(n)]
        for r in range(n):
            res = blocks[0]
            for e in range(1, n):
                res = jnp.where(grp == (r + e) % n, blocks[e], res)
            res = pltpu.roll(res, ((n - r) % n) * group, 1)
            rows32[c, pl.ds(q * n + r, nk, stride=nx), :] = res
        return 0

    lax.fori_loop(0, comps * nq, finish, 0)
    for c in range(comps):
        out[c] = rows32[c].astype(BF16)
    fcopy.wait()
    off_res = exact(half_off, fr[:, nk:], ((1,), (1,)))
    off_out[...] = jnp.where(sub == 0, 0.0, off_res)


def on_device(n, subs, start, face_x, face_y, face_z, masses, active):
    _, comps, nk, rows, nx, nz = start.shape
    assert rows == 1 and nx % n == 0 and nz % n == 0 and n >= OV and n & (n - 1) == 0
    nq, group = nx // n, nz // n
    slots = -(-comps * nx // group)
    vm, dma = pltpu.VMEM, pltpu.SemaphoreType.DMA
    ph = STEPS + 1
    vmem = pl.BlockSpec(memory_space=pltpu.VMEM)
    big = (n, comps, nq, nk, nz)
    flat = lambda v: v.reshape(nx, nz)
    out, diag, off = pl.pallas_call(
        functools.partial(kernel, n, subs, comps, nk, nx),
        out_shape=(
            jax.ShapeDtypeStruct((comps, nk * nx, nz), BF16),
            jax.ShapeDtypeStruct((nk, nk), F32),
            jax.ShapeDtypeStruct((nk, nk), F32),
        ),
        in_specs=[vmem] * 5 + [pl.BlockSpec(memory_space=pltpu.SMEM)],
        out_specs=(vmem,) * 3,
        scratch_shapes=[
            vm(big, F32), vm(big, F32), vm(big, F32), vm(big, F32),
            vm((comps, nk * nx, nz), F32),
            vm((n, 6, nq, 8, nz), F32), vm((n, 6, nq, 8, nz), F32),
            vm((7, n, nq, 8, nz), F32),
            vm((ph, 2, slots, nk, nz), F32), vm((ph, 2, slots, nk, nz), F32),
            vm((STEPS, n, nk, 2 * nk), F32), vm((n, 2, nk, 2 * nk), F32),
            vm((n, comps, nk, nz), F32), vm((n, comps, nk, nz), F32),
            vm((nk, 2 * nk), F32), vm((nk, 2 * nk), F32),
            dma((comps, n)), dma((comps, n)), dma((n,)), dma((n,)),
            dma((ph, 2)), dma((ph, 2)), dma((ph, n)), dma((ph, n)),
            dma((n,)), dma((n,)), dma((2,)), dma((2,)),
        ],
        compiler_params=pltpu.CompilerParams(
            collective_id=0, has_side_effects=True, vmem_limit_bytes=48 * 2**20
        ),
    )(
        start.reshape(comps, nk * nx, nz),
        flat(face_x), flat(face_y), flat(face_z), flat(masses), active,
    )
    return out.reshape(start.shape), diag[None], off[None]


def solution(mesh):
    grid = P("sub", "dom", None, None)
    block = P("sub", None, None, "dom", None, None)
    return jax.shard_map(
        functools.partial(on_device, mesh.shape["dom"], mesh.shape["sub"]),
        mesh=mesh,
        in_specs=(block, grid, grid, grid, grid, P("sub")),
        out_specs=(block, P("sub", None, None), P("sub", None, None)),
        check_vma=False,
    )
```

```python
import functools

import jax
import jax.numpy as jnp
from jax import lax
from jax.experimental import pallas as pl
from jax.experimental.pallas import tpu as pltpu
from jax.sharding import PartitionSpec as P

OV = 4
STEPS = 2
MESH = pl.DeviceIdType.MESH
F32 = jnp.float32
BF16 = jnp.bfloat16


def split(v):
    hi = v.astype(BF16)
    return hi, (v - hi.astype(F32)).astype(BF16)


def nt(a, b):
    return lax.dot_general(a, b, (((1,), (1,)), ((), ())), preferred_element_type=F32)


def exact(a, b, dims):
    return lax.dot_general(
        a, b, (dims, ((), ())), precision=lax.Precision.HIGHEST, preferred_element_type=F32
    )


def kernel(
    n, subs, comps, nk, nx,
    start_hbm, fx, fy, fz, mass, active,
    out, diag_out, off_out,
    start, sbuf, vec, img, home, rows32, cs, cr, dv, hs, hr, gr, gf, us, ur, fs, fr,
    s_sem, r_sem, cs_sem, cr_sem, hs_sem, hr_sem, gs_sem, gr_sem,
    ws_sem, wr_sem, us_sem, ur_sem, in_sem,
):
    nz = fx.shape[1]
    group = nz // n
    nq = nx // n
    per = n * comps
    loads = [
        pltpu.make_async_copy(start_hbm.at[c], start.at[c], in_sem.at[c]) for c in range(comps)
    ]
    for cp in loads:
        cp.start()
    me = lax.axis_index("dom")
    sub = lax.axis_index("sub")
    peers = [lax.rem(me + d, n) for d in range(n)]
    right, left = peers[1], peers[n - 1]
    next_sub, prev_sub = lax.rem(sub + 1, subs), lax.rem(sub + subs - 1, subs)

    barrier = pltpu.get_barrier_semaphore()
    for d in range(1, n):
        pl.semaphore_signal(barrier, inc=1, device_id=(sub, peers[d]), device_id_type=MESH)
    for s in (next_sub, prev_sub):
        pl.semaphore_signal(barrier, inc=1, device_id=(s, me), device_id_type=MESH)

    a = active[0]
    lane = lax.broadcasted_iota(jnp.int32, (1, nz), 1)
    grp = lane // group
    zin = lane - grp * group

    pi = lax.broadcasted_iota(jnp.int32, (nx, nz), 0)
    zi = lax.broadcasted_iota(jnp.int32, (nx, nz), 1)
    kx = jnp.where(pi + 1 < a, fx[...], 0.0)
    ky = jnp.where((pi < a) & (me + 1 < n), fy[...], 0.0)
    kz = jnp.where((pi < a) & (zi + 1 < nz), fz[...], 0.0)
    lx = jnp.where(pi == 0, 0.0, pltpu.roll(kx, 1, 0))
    lz = jnp.where(zi == 0, 0.0, pltpu.roll(kz, 1, 1))
    coefs = (kx, lx, ky, kz, lz, mass[...])

    def regroup(blocks, e):
        res = blocks[0]
        for r in range(1, n):
            res = jnp.where(grp == lax.rem(e + r, n), blocks[r], res)
        return pltpu.roll(res, lax.rem(n - e, n) * group, 1)

    for ai, arr in enumerate(coefs):
        for q in range(nq):
            blocks = [
                pltpu.roll(jnp.broadcast_to(arr[q * n + r : q * n + r + 1], (8, nz)), r * group, 1)
                for r in range(n)
            ]
            for d in range(n):
                res = regroup(blocks, peers[d])
                if d == 0:
                    cr[me, ai, q] = res
                else:
                    cs[d, ai, q] = res

    pl.semaphore_wait(barrier, n - 1 + 2)

    def to_peer(src, dst, ss, rs, d):
        return pltpu.make_async_remote_copy(
            src_ref=src, dst_ref=dst, send_sem=ss, recv_sem=rs,
            device_id=(sub, peers[d]), device_id_type=MESH,
        )

    def to_next(src, dst, ss, rs):
        return pltpu.make_async_remote_copy(
            src_ref=src, dst_ref=dst, send_sem=ss, recv_sem=rs,
            device_id=(next_sub, me), device_id_type=MESH,
        )

    coef_copies = [
        to_peer(cs.at[d], cr.at[me], cs_sem.at[d], cr_sem.at[d], d) for d in range(1, n)
    ]
    for cp in coef_copies:
        cp.start()

    vec_copies = []
    for c in range(comps):
        loads[c].wait()

        def pack(q, _, c=c):
            blocks = []
            for r in range(n):
                x = q * n + r
                v = start[c, pl.ds(x, nk, stride=nx), :]
                blocks.append(pltpu.roll(jnp.where(x < a, v, 0.0), r * group, 1))
            for d in range(n):
                res = regroup(blocks, peers[d])
                if d == 0:
                    vec[me, c, q] = res
                else:
                    sbuf[d, c, q] = res
            return 0
        lax.fori_loop(0, nq, pack, 0)
        for d in range(1, n):
            cp = to_peer(sbuf.at[d, c], vec.at[me, c], s_sem.at[c, d], r_sem.at[c, d], d)
            cp.start()
            vec_copies.append(cp)

    for cp in coef_copies:
        cp.wait()

    for y in range(n):
        for q in range(nq):
            plane = q * n + grp
            ckx, clx, cky, ckz, clz, cm = (cr[y, ai, q] for ai in range(6))
            ly = cr[y - 1, 2, q] if y else jnp.zeros_like(cky)
            total = ckx + clx + cky + ly + ckz + clz
            unity = jnp.clip(
                jnp.minimum(plane + 1, a - plane).astype(F32) / (OV + 1), 0.0, 1.0
            )
            unity = jnp.broadcast_to(unity, total.shape)
            half = 0.5 / (total + cm)
            b = cm * unity * unity
            tail = ((plane >= a - OV) & (plane < a)).astype(F32)
            for i, arr in enumerate((total, ly, half, half * b, b, unity, jnp.broadcast_to(tail, total.shape))):
                dv[i, y, q] = arr

    for cp in vec_copies:
        cp.wait()

    def halo_copies(p):
        return (
            to_peer(hs.at[p, 0], hr.at[p, 0], hs_sem.at[p, 0], hr_sem.at[p, 0], n - 1),
            to_peer(hs.at[p, 1], hr.at[p, 1], hs_sem.at[p, 1], hr_sem.at[p, 1], 1),
        )

    def put_halo(p, y, c, q, v):
        b = (y * comps + c) * nq + q
        slot = lax.div(b, group)
        pos = b - slot * group
        lo = pltpu.roll(v, pos, 1)
        hi = pltpu.roll(v, lax.rem(pos + nz + 1 - group, nz), 1)
        here = zin == pos
        hs[p, 0, slot] = jnp.where(here, lo, hs[p, 0, slot])
        hs[p, 1, slot] = jnp.where(here, hi, hs[p, 1, slot])

    def row(ref, i, y, q):
        return ref[i, y, q][0:1]

    def apply_and_gram(p):
        def body(i, acc):
            y = lax.div(i, comps)
            c = i - y * comps
            yu, yd = jnp.minimum(y + 1, n - 1), jnp.maximum(y - 1, 0)
            vs = [vec[y, c, q] for q in range(nq)]
            ups = [pltpu.roll(v, nz - group, 1) for v in vs]
            downs = [pltpu.roll(v, group, 1) for v in vs]
            lefts, bvs = [], []
            for q in range(nq):
                v = vs[q]
                b = i * nq + q
                slot = lax.div(b, group)
                pos = b - slot * group
                xp = ups[q] if q + 1 == nq else jnp.where(grp == n - 1, ups[q + 1], ups[q])
                xm = downs[q] if q == 0 else jnp.where(grp == 0, downs[q - 1], downs[q])
                zp = jnp.where(
                    zin == group - 1, pltpu.roll(hr[p, 0, slot], group - 1 - pos, 1),
                    pltpu.roll(v, nz - 1, 1),
                )
                zm = jnp.where(
                    zin == 0, pltpu.roll(hr[p, 1, slot], lax.rem(nz - pos, nz), 1),
                    pltpu.roll(v, 1, 1),
                )
                def cf(ai):
                    return cr[y, ai, q][0:1]
                res = (
                    row(dv, 0, y, q) * v
                    - cf(0) * xp - cf(1) * xm
                    - cf(2) * vec[yu, c, q] - row(dv, 1, y, q) * vec[yd, c, q]
                    - cf(3) * zp - cf(4) * zm
                )
                img[y, c, q] = res
                lefts.append(res)
                bvs.append(v * (cf(5) if p == STEPS else row(dv, 4, y, q)))
            v_hi, v_lo = split(jnp.concatenate(vs, 1))
            b_hi, b_lo = split(jnp.concatenate(bvs, 1))
            a_hi, a_lo = split(jnp.concatenate(lefts, 1))
            return acc + nt(
                jnp.concatenate([v_hi, v_lo], 0),
                jnp.concatenate([b_hi, a_hi, b_lo, a_lo], 0),
            )

        acc = lax.fori_loop(0, per, body, jnp.zeros((2 * nk, 4 * nk), F32))
        return acc[:nk, : 2 * nk] + acc[:nk, 2 * nk :] + acc[nk:, : 2 * nk]

    def spread(ref, phase):
        copies = [
            to_peer(ref.at[me], ref.at[me], gs_sem.at[phase, d], gr_sem.at[phase, d], d)
            for d in range(1, n)
        ]
        for cp in copies:
            cp.start()
        return copies

    def collect(ref, copies):
        for cp in copies:
            cp.wait()
        total = ref[0]
        for y in range(1, n):
            total = total + ref[y]
        return total

    hs[...] = jnp.zeros_like(hs)
    ri = lax.broadcasted_iota(jnp.int32, (nk, 1), 0)

    def pair(m, j):
        top, low = m[j : j + 1, :], m[j + 1 : j + 2, :]
        return top, low, top[:, j : j + 1], top[:, j + 1 : j + 2], low[:, j + 1 : j + 2]

    def pack_halo(i, _):
        y = lax.div(i, comps)
        c = i - y * comps
        for q in range(nq):
            put_halo(0, y, c, q, vec[y, c, q])
        return 0

    lax.fori_loop(0, per, pack_halo, 0)

    for p in range(STEPS):
        copies = halo_copies(p)
        for cp in copies:
            cp.start()
        for cp in copies:
            cp.wait()
        gr[p, me] = apply_and_gram(p)
        m = collect(gr.at[p], spread(gr.at[p], p))
        for j in range(0, nk, 2):
            top, low, p00, p01, p11 = pair(m, j)
            inv = 1.0 / (p00 * p11 - p01 * p01)
            new_top = (p11 * inv) * top - (p01 * inv) * low
            new_low = (p00 * inv) * low - (p01 * inv) * top
            rest = m - m[:, j : j + 1] * new_top - m[:, j + 1 : j + 2] * new_low
            m = jnp.where(ri == j, new_top, jnp.where(ri == j + 1, new_low, rest))
        xt = m.T[nk:, :]
        x_hi, x_lo = split(xt)
        x3 = jnp.concatenate([x_hi, x_lo, x_hi], 1)

        def update(i, _, p=p, x3=x3):
            y = lax.div(i, comps)
            c = i - y * comps
            v = jnp.concatenate([vec[y, c, q] for q in range(nq)], 1)
            v_hi, v_lo = split(v)
            mixed = jnp.dot(
                x3, jnp.concatenate([v_hi, v_hi, v_lo], 0), preferred_element_type=F32
            )
            for q in range(nq):
                new = (
                    vec[y, c, q]
                    - row(dv, 2, y, q) * img[y, c, q]
                    + row(dv, 3, y, q) * mixed[:, q * nz : (q + 1) * nz]
                )
                if p == STEPS - 1:
                    new = new * row(dv, 5, y, q)
                vec[y, c, q] = new
                put_halo(p + 1, y, c, q, new)
            return 0

        lax.fori_loop(0, per, update, 0)

    copies = halo_copies(STEPS)
    for cp in copies:
        cp.start()
    back = []
    for d in range(1, n):
        cp = to_peer(vec.at[peers[d]], home.at[me], ws_sem.at[d], wr_sem.at[d], d)
        cp.start()
        back.append(cp)
    for cp in copies:
        cp.wait()
    gr[STEPS, me] = apply_and_gram(STEPS)
    last_copies = spread(gr.at[STEPS], STEPS)

    r0 = lax.rem(a - OV, n)

    def planes(i, _):
        y = lax.div(i, comps)
        c = i - y * comps
        u = img[y, c, 0] * row(dv, 6, y, 0)
        for q in range(1, nq):
            u = u + img[y, c, q] * row(dv, 6, y, q)
        bit = 1
        while bit < n:
            moved = pltpu.roll(u, nz - bit * group, 1)
            u = jnp.where(lax.rem(lax.div(r0, bit), 2) == 1, moved, u)
            bit *= 2
        us[y, c] = u
        return 0

    lax.fori_loop(0, per, planes, 0)
    ucopy = to_next(us, ur, us_sem.at[0], ur_sem.at[0])
    ucopy.start()
    both = collect(gr.at[STEPS], last_copies)

    eye = (lax.broadcasted_iota(jnp.int32, (nk, 2 * nk), 0) + nk
           == lax.broadcasted_iota(jnp.int32, (nk, 2 * nk), 1)).astype(F32)
    right_half = lax.broadcasted_iota(jnp.int32, (nk, 2 * nk), 1) >= nk
    m = jnp.where(right_half, eye, both)
    for j in range(0, nk, 2):
        top, low, p00, p01, p11 = pair(m, j)
        ratio = p01 / p00
        second = low - ratio * top
        p_second = p11 - ratio * p01
        new_low = second / p_second
        new_top = top / p00 - ratio * new_low
        rest = m - m[:, j : j + 1] * new_top - m[:, j + 1 : j + 2] * new_low
        m = jnp.where(
            ri > j + 1,
            rest,
            jnp.where(
                ri == j,
                top * lax.rsqrt(p00),
                jnp.where(ri == j + 1, second * lax.rsqrt(p_second), m),
            ),
        )
    factor = m[:, nk:]
    fs[...] = m
    fcopy = to_next(fs, fr, us_sem.at[1], ur_sem.at[1])
    fcopy.start()
    ucopy.wait()

    def off_body(i, acc):
        y = lax.div(i, comps)
        c = i - y * comps
        w_hi, w_lo = split(jnp.where(grp < OV, vec[y, c, 0], 0.0))
        u_hi, u_lo = split(ur[y, c])
        return acc + nt(jnp.concatenate([w_hi, w_lo], 0), jnp.concatenate([u_hi, u_lo], 0))

    off = lax.fori_loop(0, per, off_body, jnp.zeros((2 * nk, 2 * nk), F32))
    off = off[:nk, :nk] + off[nk:, :nk] + off[:nk, nk:]
    gf[me] = jnp.concatenate([off, jnp.zeros_like(off)], 1)
    off_copies = spread(gf, STEPS + 1)
    diag_out[...] = exact(
        exact(factor, both[:, nk:], ((1,), (0,))), factor, ((1,), (1,))
    )

    for y_cp in back:
        y_cp.wait()
    f_hi, f_lo = split(factor)
    f3 = jnp.concatenate([f_hi, f_lo, f_hi], 1)
    home[me] = vec[me]

    def finish(i, _):
        c = lax.div(i, nq)
        q = i - c * nq
        w = jnp.concatenate([home[e, c, q] for e in range(n)], 1)
        w_hi, w_lo = split(w)
        z = jnp.dot(f3, jnp.concatenate([w_hi, w_hi, w_lo], 0), preferred_element_type=F32)
        blocks = [pltpu.roll(z[:, e * nz : (e + 1) * nz], e * group, 1) for e in range(n)]
        for r in range(n):
            res = blocks[0]
            for e in range(1, n):
                res = jnp.where(grp == (r + e) % n, blocks[e], res)
            res = pltpu.roll(res, ((n - r) % n) * group, 1)
            rows32[c, pl.ds(q * n + r, nk, stride=nx), :] = res
        return 0

    lax.fori_loop(0, comps * nq, finish, 0)
    for c in range(comps):
        out[c] = rows32[c].astype(BF16)
    fcopy.wait()
    half_off = exact(factor, collect(gf, off_copies)[:, :nk], ((1,), (0,)))
    off_res = exact(half_off, fr[:, nk:], ((1,), (1,)))
    off_out[...] = jnp.where(sub == 0, 0.0, off_res)


def on_device(n, subs, start, face_x, face_y, face_z, masses, active):
    _, comps, nk, rows, nx, nz = start.shape
    assert rows == 1 and nx % n == 0 and nz % n == 0 and n >= OV and n & (n - 1) == 0
    nq, group = nx // n, nz // n
    slots = -(-comps * nx // group)
    vm, dma = pltpu.VMEM, pltpu.SemaphoreType.DMA
    ph = STEPS + 1
    vmem = pl.BlockSpec(memory_space=pltpu.VMEM)
    big = (n, comps, nq, nk, nz)
    flat = lambda v: v.reshape(nx, nz)
    out, diag, off = pl.pallas_call(
        functools.partial(kernel, n, subs, comps, nk, nx),
        out_shape=(
            jax.ShapeDtypeStruct((comps, nk * nx, nz), BF16),
            jax.ShapeDtypeStruct((nk, nk), F32),
            jax.ShapeDtypeStruct((nk, nk), F32),
        ),
        in_specs=[pl.BlockSpec(memory_space=pltpu.HBM)] + [vmem] * 4 + [pl.BlockSpec(memory_space=pltpu.SMEM)],
        out_specs=(vmem,) * 3,
        scratch_shapes=[
            vm((comps, nk * nx, nz), F32),
            vm(big, F32), vm(big, F32), vm(big, F32), vm(big, F32),
            vm((comps, nk * nx, nz), F32),
            vm((n, 6, nq, 8, nz), F32), vm((n, 6, nq, 8, nz), F32),
            vm((7, n, nq, 8, nz), F32),
            vm((ph, 2, slots, nk, nz), F32), vm((ph, 2, slots, nk, nz), F32),
            vm((ph, n, nk, 2 * nk), F32), vm((n, nk, 2 * nk), F32),
            vm((n, comps, nk, nz), F32), vm((n, comps, nk, nz), F32),
            vm((nk, 2 * nk), F32), vm((nk, 2 * nk), F32),
            dma((comps, n)), dma((comps, n)), dma((n,)), dma((n,)),
            dma((ph, 2)), dma((ph, 2)), dma((ph + 1, n)), dma((ph + 1, n)),
            dma((n,)), dma((n,)), dma((2,)), dma((2,)), dma((comps,)),
        ],
        compiler_params=pltpu.CompilerParams(
            collective_id=0, has_side_effects=True, vmem_limit_bytes=48 * 2**20
        ),
    )(
        start.reshape(comps, nk * nx, nz),
        flat(face_x), flat(face_y), flat(face_z), flat(masses), active,
    )
    return out.reshape(start.shape), diag[None], off[None]


def solution(mesh):
    grid = P("sub", "dom", None, None)
    block = P("sub", None, None, "dom", None, None)
    return jax.shard_map(
        functools.partial(on_device, mesh.shape["dom"], mesh.shape["sub"]),
        mesh=mesh,
        in_specs=(block, grid, grid, grid, grid, P("sub")),
        out_specs=(block, P("sub", None, None), P("sub", None, None)),
        check_vma=False,
    )
```

```python
import functools

import jax
import jax.numpy as jnp
from jax import lax
from jax.experimental import pallas as pl
from jax.experimental.pallas import tpu as pltpu
from jax.sharding import PartitionSpec as P

OV = 4
STEPS = 2
MESH = pl.DeviceIdType.MESH
F32 = jnp.float32
BF16 = jnp.bfloat16


def split(v):
    hi = v.astype(BF16)
    return hi, (v - hi.astype(F32)).astype(BF16)


def nt(a, b):
    return lax.dot_general(a, b, (((1,), (1,)), ((), ())), preferred_element_type=F32)


def exact(a, b, dims):
    return lax.dot_general(
        a, b, (dims, ((), ())), precision=lax.Precision.HIGHEST, preferred_element_type=F32
    )


def kernel(
    n, subs, comps, nk, nx,
    start_hbm, fx, fy, fz, mass, active,
    out, diag_out, off_out,
    start, sbuf, vec, img, home, rows32, cs, cr, dv, hs, hr, gr, gf, us, ur, fs, fr,
    s_sem, r_sem, cs_sem, cr_sem, hs_sem, hr_sem, gs_sem, gr_sem,
    ws_sem, wr_sem, us_sem, ur_sem, in_sem,
):
    nz = fx.shape[1]
    group = nz // n
    nq = nx // n
    per = n * comps
    loads = [
        pltpu.make_async_copy(start_hbm.at[c], start.at[c], in_sem.at[c]) for c in range(comps)
    ]
    for cp in loads:
        cp.start()
    me = lax.axis_index("dom")
    sub = lax.axis_index("sub")
    peers = [lax.rem(me + d, n) for d in range(n)]
    right, left = peers[1], peers[n - 1]
    next_sub, prev_sub = lax.rem(sub + 1, subs), lax.rem(sub + subs - 1, subs)

    barrier = pltpu.get_barrier_semaphore()
    for d in range(1, n):
        pl.semaphore_signal(barrier, inc=1, device_id=(sub, peers[d]), device_id_type=MESH)
    for s in (next_sub, prev_sub):
        pl.semaphore_signal(barrier, inc=1, device_id=(s, me), device_id_type=MESH)

    a = active[0]
    lane = lax.broadcasted_iota(jnp.int32, (1, nz), 1)
    grp = lane // group
    zin = lane - grp * group

    pi = lax.broadcasted_iota(jnp.int32, (nx, nz), 0)
    zi = lax.broadcasted_iota(jnp.int32, (nx, nz), 1)
    kx = jnp.where(pi + 1 < a, fx[...], 0.0)
    ky = jnp.where((pi < a) & (me + 1 < n), fy[...], 0.0)
    kz = jnp.where((pi < a) & (zi + 1 < nz), fz[...], 0.0)
    lx = jnp.where(pi == 0, 0.0, pltpu.roll(kx, 1, 0))
    lz = jnp.where(zi == 0, 0.0, pltpu.roll(kz, 1, 1))
    coefs = (kx, lx, ky, kz, lz, mass[...])

    def regroup(blocks, e):
        res = blocks[0]
        for r in range(1, n):
            res = jnp.where(grp == lax.rem(e + r, n), blocks[r], res)
        return pltpu.roll(res, lax.rem(n - e, n) * group, 1)

    for ai, arr in enumerate(coefs):
        for q in range(nq):
            blocks = [
                pltpu.roll(jnp.broadcast_to(arr[q * n + r : q * n + r + 1], (8, nz)), r * group, 1)
                for r in range(n)
            ]
            for d in range(n):
                res = regroup(blocks, peers[d])
                if d == 0:
                    cr[me, ai, q] = res
                else:
                    cs[d, ai, q] = res

    pl.semaphore_wait(barrier, n - 1 + 2)

    def to_peer(src, dst, ss, rs, d):
        return pltpu.make_async_remote_copy(
            src_ref=src, dst_ref=dst, send_sem=ss, recv_sem=rs,
            device_id=(sub, peers[d]), device_id_type=MESH,
        )

    def to_next(src, dst, ss, rs):
        return pltpu.make_async_remote_copy(
            src_ref=src, dst_ref=dst, send_sem=ss, recv_sem=rs,
            device_id=(next_sub, me), device_id_type=MESH,
        )

    coef_copies = [
        to_peer(cs.at[d], cr.at[me], cs_sem.at[d], cr_sem.at[d], d) for d in range(1, n)
    ]
    for cp in coef_copies:
        cp.start()

    vec_copies = []
    for c in range(comps):
        loads[c].wait()

        def pack(q, _, c=c):
            blocks = []
            for r in range(n):
                x = q * n + r
                v = start[c, pl.ds(x, nk, stride=nx), :]
                blocks.append(pltpu.roll(jnp.where(x < a, v, 0.0), r * group, 1))
            for d in range(n):
                res = regroup(blocks, peers[d])
                if d == 0:
                    vec[me, c, q] = res
                else:
                    sbuf[d, c, q] = res
            return 0
        lax.fori_loop(0, nq, pack, 0)
        for d in range(1, n):
            cp = to_peer(sbuf.at[d, c], vec.at[me, c], s_sem.at[c, d], r_sem.at[c, d], d)
            cp.start()
            vec_copies.append(cp)

    for cp in coef_copies:
        cp.wait()

    for y in range(n):
        for q in range(nq):
            plane = q * n + grp
            ckx, clx, cky, ckz, clz, cm = (cr[y, ai, q] for ai in range(6))
            ly = cr[y - 1, 2, q] if y else jnp.zeros_like(cky)
            total = ckx + clx + cky + ly + ckz + clz
            unity = jnp.clip(
                jnp.minimum(plane + 1, a - plane).astype(F32) / (OV + 1), 0.0, 1.0
            )
            unity = jnp.broadcast_to(unity, total.shape)
            half = 0.5 / (total + cm)
            b = cm * unity * unity
            tail = ((plane >= a - OV) & (plane < a)).astype(F32)
            for i, arr in enumerate((total, ly, half, half * b, b, unity, jnp.broadcast_to(tail, total.shape))):
                dv[i, y, q] = arr

    for cp in vec_copies:
        cp.wait()

    def halo_copies(p):
        return (
            to_peer(hs.at[p, 0], hr.at[p, 0], hs_sem.at[p, 0], hr_sem.at[p, 0], n - 1),
            to_peer(hs.at[p, 1], hr.at[p, 1], hs_sem.at[p, 1], hr_sem.at[p, 1], 1),
        )

    def put_halo(p, y, c, q, v):
        b = (y * comps + c) * nq + q
        slot = lax.div(b, group)
        pos = b - slot * group
        lo = pltpu.roll(v, pos, 1)
        hi = pltpu.roll(v, lax.rem(pos + nz + 1 - group, nz), 1)
        here = zin == pos
        hs[p, 0, slot] = jnp.where(here, lo, hs[p, 0, slot])
        hs[p, 1, slot] = jnp.where(here, hi, hs[p, 1, slot])

    def row(ref, i, y, q):
        return ref[i, y, q][0:1]

    def apply_and_gram(p):
        def body(i, acc):
            y = lax.div(i, comps)
            c = i - y * comps
            yu, yd = jnp.minimum(y + 1, n - 1), jnp.maximum(y - 1, 0)
            vs = [vec[y, c, q] for q in range(nq)]
            ups = [pltpu.roll(v, nz - group, 1) for v in vs]
            downs = [pltpu.roll(v, group, 1) for v in vs]
            lefts, bvs = [], []
            for q in range(nq):
                v = vs[q]
                b = i * nq + q
                slot = lax.div(b, group)
                pos = b - slot * group
                xp = ups[q] if q + 1 == nq else jnp.where(grp == n - 1, ups[q + 1], ups[q])
                xm = downs[q] if q == 0 else jnp.where(grp == 0, downs[q - 1], downs[q])
                zp = jnp.where(
                    zin == group - 1, pltpu.roll(hr[p, 0, slot], group - 1 - pos, 1),
                    pltpu.roll(v, nz - 1, 1),
                )
                zm = jnp.where(
                    zin == 0, pltpu.roll(hr[p, 1, slot], lax.rem(nz - pos, nz), 1),
                    pltpu.roll(v, 1, 1),
                )
                def cf(ai):
                    return cr[y, ai, q][0:1]
                res = (
                    row(dv, 0, y, q) * v
                    - cf(0) * xp - cf(1) * xm
                    - cf(2) * vec[yu, c, q] - row(dv, 1, y, q) * vec[yd, c, q]
                    - cf(3) * zp - cf(4) * zm
                )
                img[y, c, q] = res
                lefts.append(res)
                bvs.append(v * (cf(5) if p == STEPS else row(dv, 4, y, q)))
            v_hi, v_lo = split(jnp.concatenate(vs, 1))
            b_hi, b_lo = split(jnp.concatenate(bvs, 1))
            a_hi, a_lo = split(jnp.concatenate(lefts, 1))
            return acc + nt(
                jnp.concatenate([v_hi, v_lo], 0),
                jnp.concatenate([b_hi, a_hi, b_lo, a_lo], 0),
            )

        acc = lax.fori_loop(0, per, body, jnp.zeros((2 * nk, 4 * nk), F32))
        return acc[:nk, : 2 * nk] + acc[:nk, 2 * nk :] + acc[nk:, : 2 * nk]

    def spread(ref, phase):
        copies = [
            to_peer(ref.at[me], ref.at[me], gs_sem.at[phase, d], gr_sem.at[phase, d], d)
            for d in range(1, n)
        ]
        for cp in copies:
            cp.start()
        return copies

    def collect(ref, copies):
        for cp in copies:
            cp.wait()
        total = ref[0]
        for y in range(1, n):
            total = total + ref[y]
        return total

    hs[...] = jnp.zeros_like(hs)
    ri = lax.broadcasted_iota(jnp.int32, (nk, 1), 0)

    def pack_halo(i, _):
        y = lax.div(i, comps)
        c = i - y * comps
        for q in range(nq):
            put_halo(0, y, c, q, vec[y, c, q])
        return 0

    lax.fori_loop(0, per, pack_halo, 0)

    for p in range(STEPS):
        copies = halo_copies(p)
        for cp in copies:
            cp.start()
        for cp in copies:
            cp.wait()
        gr[p, me] = apply_and_gram(p)
        m = collect(gr.at[p], spread(gr.at[p], p))
        for j in range(nk):
            piv = m[j : j + 1, j : j + 1]
            line = m[j : j + 1, :] / piv
            m = jnp.where(ri == j, line, m - m[:, j : j + 1] * line)
        xt = m.T[nk:, :]
        x_hi, x_lo = split(xt)
        x3 = jnp.concatenate([x_hi, x_lo, x_hi], 1)

        def update(i, _, p=p, x3=x3):
            y = lax.div(i, comps)
            c = i - y * comps
            v = jnp.concatenate([vec[y, c, q] for q in range(nq)], 1)
            v_hi, v_lo = split(v)
            mixed = jnp.dot(
                x3, jnp.concatenate([v_hi, v_hi, v_lo], 0), preferred_element_type=F32
            )
            for q in range(nq):
                new = (
                    vec[y, c, q]
                    - row(dv, 2, y, q) * img[y, c, q]
                    + row(dv, 3, y, q) * mixed[:, q * nz : (q + 1) * nz]
                )
                if p == STEPS - 1:
                    new = new * row(dv, 5, y, q)
                vec[y, c, q] = new
                put_halo(p + 1, y, c, q, new)
            return 0

        lax.fori_loop(0, per, update, 0)

    copies = halo_copies(STEPS)
    for cp in copies:
        cp.start()
    back = []
    for d in range(1, n):
        cp = to_peer(vec.at[peers[d]], home.at[me], ws_sem.at[d], wr_sem.at[d], d)
        cp.start()
        back.append(cp)
    for cp in copies:
        cp.wait()
    gr[STEPS, me] = apply_and_gram(STEPS)
    last_copies = spread(gr.at[STEPS], STEPS)

    r0 = lax.rem(a - OV, n)

    def planes(i, _):
        y = lax.div(i, comps)
        c = i - y * comps
        u = img[y, c, 0] * row(dv, 6, y, 0)
        for q in range(1, nq):
            u = u + img[y, c, q] * row(dv, 6, y, q)
        bit = 1
        while bit < n:
            moved = pltpu.roll(u, nz - bit * group, 1)
            u = jnp.where(lax.rem(lax.div(r0, bit), 2) == 1, moved, u)
            bit *= 2
        us[y, c] = u
        return 0

    lax.fori_loop(0, per, planes, 0)
    ucopy = to_next(us, ur, us_sem.at[0], ur_sem.at[0])
    ucopy.start()
    both = collect(gr.at[STEPS], last_copies)

    eye = (lax.broadcasted_iota(jnp.int32, (nk, 2 * nk), 0) + nk
           == lax.broadcasted_iota(jnp.int32, (nk, 2 * nk), 1)).astype(F32)
    right_half = lax.broadcasted_iota(jnp.int32, (nk, 2 * nk), 1) >= nk
    m = jnp.where(right_half, eye, both)
    for j in range(nk):
        piv = m[j : j + 1, j : j + 1]
        line = m[j : j + 1, :]
        inv = 1.0 / piv
        m = jnp.where(
            ri > j, m - m[:, j : j + 1] * (line * inv), jnp.where(ri == j, line * lax.rsqrt(piv), m)
        )
    factor = m[:, nk:]
    fs[...] = m
    fcopy = to_next(fs, fr, us_sem.at[1], ur_sem.at[1])
    fcopy.start()
    ucopy.wait()

    def off_body(i, acc):
        y = lax.div(i, comps)
        c = i - y * comps
        w_hi, w_lo = split(jnp.where(grp < OV, vec[y, c, 0], 0.0))
        u_hi, u_lo = split(ur[y, c])
        return acc + nt(jnp.concatenate([w_hi, w_lo], 0), jnp.concatenate([u_hi, u_lo], 0))

    off = lax.fori_loop(0, per, off_body, jnp.zeros((2 * nk, 2 * nk), F32))
    off = off[:nk, :nk] + off[nk:, :nk] + off[:nk, nk:]
    gf[me] = jnp.concatenate([off, jnp.zeros_like(off)], 1)
    off_copies = spread(gf, STEPS + 1)
    diag_out[...] = exact(
        exact(factor, both[:, nk:], ((1,), (0,))), factor, ((1,), (1,))
    )

    for y_cp in back:
        y_cp.wait()
    f_hi, f_lo = split(factor)
    f3 = jnp.concatenate([f_hi, f_lo, f_hi], 1)
    home[me] = vec[me]

    def finish(i, _):
        c = lax.div(i, nq)
        q = i - c * nq
        w = jnp.concatenate([home[e, c, q] for e in range(n)], 1)
        w_hi, w_lo = split(w)
        z = jnp.dot(f3, jnp.concatenate([w_hi, w_hi, w_lo], 0), preferred_element_type=F32)
        blocks = [pltpu.roll(z[:, e * nz : (e + 1) * nz], e * group, 1) for e in range(n)]
        for r in range(n):
            res = blocks[0]
            for e in range(1, n):
                res = jnp.where(grp == (r + e) % n, blocks[e], res)
            res = pltpu.roll(res, ((n - r) % n) * group, 1)
            rows32[c, pl.ds(q * n + r, nk, stride=nx), :] = res
        return 0

    lax.fori_loop(0, comps * nq, finish, 0)
    for c in range(comps):
        out[c] = rows32[c].astype(BF16)
    fcopy.wait()
    half_off = exact(factor, collect(gf, off_copies)[:, :nk], ((1,), (0,)))
    off_res = exact(half_off, fr[:, nk:], ((1,), (1,)))
    off_out[...] = jnp.where(sub == 0, 0.0, off_res)


def on_device(n, subs, start, face_x, face_y, face_z, masses, active):
    _, comps, nk, rows, nx, nz = start.shape
    assert rows == 1 and nx % n == 0 and nz % n == 0 and n >= OV and n & (n - 1) == 0
    nq, group = nx // n, nz // n
    slots = -(-comps * nx // group)
    vm, dma = pltpu.VMEM, pltpu.SemaphoreType.DMA
    ph = STEPS + 1
    vmem = pl.BlockSpec(memory_space=pltpu.VMEM)
    big = (n, comps, nq, nk, nz)
    flat = lambda v: v.reshape(nx, nz)
    out, diag, off = pl.pallas_call(
        functools.partial(kernel, n, subs, comps, nk, nx),
        out_shape=(
            jax.ShapeDtypeStruct((comps, nk * nx, nz), BF16),
            jax.ShapeDtypeStruct((nk, nk), F32),
            jax.ShapeDtypeStruct((nk, nk), F32),
        ),
        in_specs=[pl.BlockSpec(memory_space=pltpu.HBM)] + [vmem] * 4 + [pl.BlockSpec(memory_space=pltpu.SMEM)],
        out_specs=(vmem,) * 3,
        scratch_shapes=[
            vm((comps, nk * nx, nz), F32),
            vm(big, F32), vm(big, F32), vm(big, F32), vm(big, F32),
            vm((comps, nk * nx, nz), F32),
            vm((n, 6, nq, 8, nz), F32), vm((n, 6, nq, 8, nz), F32),
            vm((7, n, nq, 8, nz), F32),
            vm((ph, 2, slots, nk, nz), F32), vm((ph, 2, slots, nk, nz), F32),
            vm((ph, n, nk, 2 * nk), F32), vm((n, nk, 2 * nk), F32),
            vm((n, comps, nk, nz), F32), vm((n, comps, nk, nz), F32),
            vm((nk, 2 * nk), F32), vm((nk, 2 * nk), F32),
            dma((comps, n)), dma((comps, n)), dma((n,)), dma((n,)),
            dma((ph, 2)), dma((ph, 2)), dma((ph + 1, n)), dma((ph + 1, n)),
            dma((n,)), dma((n,)), dma((2,)), dma((2,)), dma((comps,)),
        ],
        compiler_params=pltpu.CompilerParams(
            collective_id=0, has_side_effects=True, vmem_limit_bytes=48 * 2**20
        ),
    )(
        start.reshape(comps, nk * nx, nz),
        flat(face_x), flat(face_y), flat(face_z), flat(masses), active,
    )
    return out.reshape(start.shape), diag[None], off[None]


def solution(mesh):
    grid = P("sub", "dom", None, None)
    block = P("sub", None, None, "dom", None, None)
    return jax.shard_map(
        functools.partial(on_device, mesh.shape["dom"], mesh.shape["sub"]),
        mesh=mesh,
        in_specs=(block, grid, grid, grid, grid, P("sub")),
        out_specs=(block, P("sub", None, None), P("sub", None, None)),
        check_vma=False,
    )
```
